128 devices in a mesh: seq: 64 (over x, y, z_lo, core), head: 2 (over z_hi).
Axes of the slice: x: 4, y: 4, z: 4 (z_hi: 2, z_lo: 2; z = z_hi * 2 + z_lo), core: 2. Of those that a mesh axis runs over, the one named last changes fastest.
Arguments:
- queries: bfloat16 [2, 32768, 1024], P(None, 'seq', 'head'), may hold values from -40 to 40, as said below
- keys: bfloat16 [2, 32768, 1024], P(None, 'seq', 'head'), may hold values from -40 to 40, as said below
- values: bfloat16 [2, 32768, 1024], P(None, 'seq', 'head'), may hold values from -6 to 6
- token_rate: float32 [2, 4, 32768], P(None, 'head', 'seq'), may hold values from 0.05 to 1
- step_size: float32 [4], P('head'), may hold values from 0.5 to 1
- w_gate: float32 [4, 512, 256], P('head'), may hold values from -0.375 to 0.375
- w_up: float32 [4, 512, 256], P('head'), may hold values from -0.375 to 0.375
- w_down: float32 [4, 256, 512], P('head'), may hold values from -0.25 to 0.25
- w_out: bfloat16 [1024, 1024], P('head'), may hold values from -0.1875 to 0.1875
Outputs:
- mixed: bfloat16 [2, 32768, 1024], P(None, 'seq', 'head')
- gate_state: float32 [4, 512, 256], P('head')
- up_state: float32 [4, 512, 256], P('head')
- down_state: float32 [4, 256, 512], P('head')
The draws below stay inside these ranges and needn't reach their ends.
Inputs may be any that keep to these rules, and one draw needn't show every extreme that they name: `queries`: Real-valued entries. `keys`: Real-valued entries.
All inputs are finite; a program needn't handle non-finite values.
Results may differ from the reference program's by a relative error of at most 0.028.
Values may be sent and summed in bfloat16 or wider, within the bound.
A program may use at most 128 MiB of HBM per device.

```python
import math
import jax
import jax.numpy as jnp
from jax import lax

D = 1024
H = 4
DH = 256
FH = 512
WIN = 256
NS_STEPS = 5
SEGMENTS = 2
CT = 32768
N_HEAD = 2


def draw_queries(key, part):
    key = jax.random.fold_in(key, 1)
    drawn_rows = jax.random.normal(key, (SEGMENTS, CT, D), jnp.float32)
    return drawn_rows.astype(jnp.bfloat16)


def draw_keys(key, part):
    key = jax.random.fold_in(key, 2)
    drawn_rows = jax.random.normal(key, (SEGMENTS, CT, D), jnp.float32)
    return drawn_rows.astype(jnp.bfloat16)


def levels(key, shape, split, least, high):
    loudness = 1.0
    for position, blocks in split:
        steps = jax.random.uniform(jax.random.fold_in(jax.random.fold_in(key, 6), position), (blocks,), jnp.float32, least / len(split), high / len(split))
        loudness = loudness * jnp.repeat(jnp.exp(steps), shape[position] // blocks).reshape((-1,) + (1,) * (len(shape) - 1 - position))
    return loudness


def gaussian(rng, shape, scale, reach, pieces=(), kind=jnp.bfloat16):
    gain = levels(rng, shape, pieces, -0.22, 0.18) if pieces else 1.0
    entries = jax.random.normal(rng, shape, jnp.float32) * scale * gain
    return jnp.minimum(jnp.maximum(entries, -reach), reach).astype(kind)


def setup_inputs(seed: int = 0) -> dict:
    splits = jax.random.split(jax.random.key(seed), 10)
    return {
        "queries": draw_queries(jax.random.fold_in(splits[9], 71), 0),
        "keys": draw_keys(jax.random.fold_in(splits[9], 71), 0),
        "values": gaussian(splits[2], (SEGMENTS, CT, D), 1.0, 6.0, ((1, 64), (2, 2))),
        "token_rate": jnp.clip(jnp.exp(math.log(1.0) - 2.9957323 * jax.random.uniform(splits[3], (SEGMENTS, H, CT), jnp.float32) ** levels(splits[3], (SEGMENTS, H, CT), ((1, 2), (2, 64)), -0.2, 0.2)), 0.05, 1.0),
        "step_size": jnp.clip(jnp.exp(math.log(1.0) - 0.6931472 * jax.random.uniform(splits[4], (H,), jnp.float32) ** levels(splits[4], (H,), ((0, 2),), -0.2, 0.2)), 0.5, 1.0),
        "w_gate": gaussian(splits[5], (H, FH, DH), DH ** -0.5, 0.375, ((0, 2),), jnp.float32),
        "w_up": gaussian(splits[6], (H, FH, DH), DH ** -0.5, 0.375, ((0, 2),), jnp.float32),
        "w_down": gaussian(splits[7], (H, DH, FH), FH ** -0.5, 0.25, ((0, 2),), jnp.float32),
        "w_out": gaussian(splits[8], (D, D), D ** -0.5, 0.1875, ((0, 2),)),
    }


coef_a = 3.4445
coef_b = -4.775
coef_c = 2.0315
tiny = 1e-07
highest = lax.Precision.HIGHEST

def window_segment(query_rows, key_rows, value_rows):
    total_rows = query_rows.shape[0]
    block_rows = min(512, total_rows)
    query_heads = query_rows.reshape(total_rows, H, DH)
    padding = jnp.zeros((WIN, H, DH), key_rows.dtype)
    key_heads = jnp.concatenate([padding, key_rows.reshape(total_rows, H, DH)], axis=0)
    value_heads = jnp.concatenate([padding, value_rows.reshape(total_rows, H, DH)], axis=0)
    row_ids = lax.broadcasted_iota(jnp.int32, (block_rows, block_rows + WIN), 0)
    col_ids = lax.broadcasted_iota(jnp.int32, (block_rows, block_rows + WIN), 1)
    distance = row_ids + WIN - col_ids

    def one_block(block_index):
        first_row = (block_index * block_rows).astype(jnp.int32)
        query_block = lax.dynamic_slice_in_dim(query_heads, first_row, block_rows, 0).astype(jnp.float32)
        key_block = lax.dynamic_slice_in_dim(key_heads, first_row, block_rows + WIN, 0).astype(jnp.float32)
        value_block = lax.dynamic_slice_in_dim(value_heads, first_row, block_rows + WIN, 0).astype(jnp.float32)
        scores = jnp.einsum('qhd,khd->hqk', query_block, key_block, precision=highest) / math.sqrt(DH)
        allowed = (distance >= 0) & (distance < WIN) & (first_row + col_ids - WIN >= 0)
        scores = jnp.where(allowed[None], scores, -1e+30)
        row_max = lax.optimization_barrier(jnp.max(scores, axis=-1, keepdims=True))
        weights = jnp.exp(scores - row_max)
        probs = lax.optimization_barrier((weights / lax.optimization_barrier(jnp.sum(weights, axis=-1, keepdims=True))).astype(jnp.bfloat16))
        return jnp.einsum('hqk,khd->qhd', probs.astype(jnp.float32), value_block, precision=highest)
    outputs = lax.map(one_block, jnp.arange(total_rows // block_rows, dtype=jnp.int32))
    return outputs.reshape(total_rows, H * DH)

def orthogonal(grad):
    current = grad / (jnp.sqrt(jnp.sum(grad * grad)) + tiny)
    for step_index in range(NS_STEPS):
        gram = jnp.dot(current.T, current, precision=highest)
        mixer = coef_b * gram + coef_c * jnp.dot(gram, gram, precision=highest)
        current = coef_a * current + jnp.dot(current, mixer, precision=highest)
    return current

def head_update(key_rows, value_rows, rate_row, gate_copy, up_copy, down_copy):
    gate_pre = jnp.dot(key_rows, gate_copy.T, preferred_element_type=jnp.float32)
    up_pre = jnp.dot(key_rows, up_copy.T, preferred_element_type=jnp.float32)
    sigmoid_gate = jax.nn.sigmoid(gate_pre)
    gate_act = gate_pre * sigmoid_gate
    hidden_act = (gate_act * up_pre).astype(jnp.bfloat16)
    error_rows = (-(rate_row[:, None] * value_rows.astype(jnp.float32))).astype(jnp.bfloat16)
    back_act = jnp.dot(error_rows, down_copy, preferred_element_type=jnp.float32)
    grad_gate_pre = (back_act * up_pre * sigmoid_gate * (1.0 + gate_pre * (1.0 - sigmoid_gate))).astype(jnp.bfloat16)
    grad_up_pre = (back_act * gate_act).astype(jnp.bfloat16)
    grad_gate = jnp.dot(grad_gate_pre.T, key_rows, preferred_element_type=jnp.float32)
    grad_up = jnp.dot(grad_up_pre.T, key_rows, preferred_element_type=jnp.float32)
    grad_down = jnp.dot(hidden_act.T, error_rows, preferred_element_type=jnp.float32)
    return (orthogonal(grad_gate), orthogonal(grad_up), orthogonal(grad_down))

def reference(queries, keys, values, token_rate, step_size, w_gate, w_up, w_down, w_out):
    gate_state, up_state, down_state = (w_gate, w_up, w_down)
    combined_parts = []
    for seg_index in range(SEGMENTS):
        attended = window_segment(queries[seg_index], keys[seg_index], values[seg_index])
        gate_list, up_list, down_list, fast_list = ([], [], [], [])
        for head_index in range(H):
            col_slice = slice(head_index * DH, (head_index + 1) * DH)
            upd_gate, upd_up, upd_down = head_update(keys[seg_index][:, col_slice], values[seg_index][:, col_slice], token_rate[seg_index, head_index], gate_state[head_index].astype(jnp.bfloat16), up_state[head_index].astype(jnp.bfloat16), down_state[head_index].astype(jnp.bfloat16))
            new_gate = gate_state[head_index] - step_size[head_index] * upd_gate
            new_up = up_state[head_index] - step_size[head_index] * upd_up
            new_down = down_state[head_index] - step_size[head_index] * upd_down.T
            query_rows = queries[seg_index][:, col_slice]
            gate_copy = new_gate.astype(jnp.bfloat16)
            up_copy = new_up.astype(jnp.bfloat16)
            down_copy = new_down.astype(jnp.bfloat16)
            hidden_act = (jax.nn.silu(jnp.dot(query_rows, gate_copy.T, preferred_element_type=jnp.float32)) * jnp.dot(query_rows, up_copy.T, preferred_element_type=jnp.float32)).astype(jnp.bfloat16)
            fast_list.append(jnp.dot(hidden_act, down_copy.T, preferred_element_type=jnp.float32))
            gate_list.append(new_gate)
            up_list.append(new_up)
            down_list.append(new_down)
        gate_state = jnp.stack(gate_list)
        up_state = jnp.stack(up_list)
        down_state = jnp.stack(down_list)
        fast_out = jnp.concatenate(fast_list, axis=1)
        combined_parts.append((attended + fast_out).astype(jnp.bfloat16))
    combined = jnp.stack(combined_parts).reshape(SEGMENTS * CT, D)
    group_width = D // N_HEAD
    mixed = jnp.zeros((SEGMENTS * CT, D), jnp.float32)
    for group_index in range(N_HEAD):
        lower = group_index * group_width
        partial_out = jnp.dot(combined[:, lower:lower + group_width], w_out[lower:lower + group_width], preferred_element_type=jnp.float32)
        rounded = lax.optimization_barrier(partial_out.astype(jnp.bfloat16))
        mixed = mixed + rounded.astype(jnp.float32)
    return (mixed.astype(jnp.bfloat16).reshape(SEGMENTS, CT, D), gate_state, up_state, down_state)
```

```python
import functools

import jax
import jax.numpy as jnp
from jax import lax
from jax.experimental import pallas as pl
from jax.experimental.pallas import tpu as pltpu
from jax.sharding import PartitionSpec as P

F32 = jnp.float32
BF = jnp.bfloat16
MESH = pl.DeviceIdType.MESH

DH = 256
FH = 512
WIN = 256
T = 512
TC = 2 * T
SEG = 2
BLK = 256
coef_a = 3.4445
coef_b = -4.775
coef_c = 2.0315
tiny = 1e-07

SINGLE_STEPS = 3
SPLIT_STEPS = 2


def nn(a, b):
    return jnp.dot(a, b, preferred_element_type=F32)


def nt(a, b):
    return lax.dot_general(a, b, (((1,), (1,)), ((), ())), preferred_element_type=F32)


def tn(a, b):
    return lax.dot_general(a, b, (((0,), (0,)), ((), ())), preferred_element_type=F32)


def sigmoid(v):
    return 1.0 / (1.0 + jnp.exp(-v))


def split(a):
    high = a.astype(BF)
    return high, (a - high.astype(F32)).astype(BF)


def kernel(
    q_ref, k_ref, v_ref, rate_ref, step_ref, wg_ref, wu_ref, wd_ref, wo_ref,
    mixed_ref, gate_ref, up_ref, down_ref,
    qb, kb, vb, rates, rate_send, w, wb, wdb, wo, act, d1, d3, g32, gb, rsr, arb, gf, xs,
    att, cs, cb, zs, zo, zr, mx,
    loc_sem, w_sem, wo_sem, d2d_s, d2d_r, rate_s, rate_r, halo_s, halo_r,
    rs_s, rs_r, ar_s, ar_r, ag_s, ag_r, cs_s, cs_r, zs_s, zs_r, st_s, st_r, out_sem,
):
    seq = lax.axis_index("seq")
    hg = lax.axis_index("head")
    c = lax.rem(seq, 2)
    z = lax.rem(seq // 2, 2)
    y = lax.rem(seq // 4, 4)
    x = seq // 16
    oc = 1 - c
    chip = seq // 2

    def at(px, py, pz, pc=None):
        return {"seq": ((px * 4 + py) * 2 + pz) * 2 + (c if pc is None else pc)}

    sibling = at(x, y, z, oc)
    across = {"head": 1 - hg}
    next_chip = {"seq": lax.rem(chip + 1, 32) * 2 + c}
    prev_chip = {"seq": lax.rem(chip + 31, 32) * 2 + c}

    def group8(m, k):
        r, b = k // 2, k % 2
        if m == 0:
            py, pz = lax.rem(y + r, 4), lax.rem(z + b, 2)
            return at(x, py, pz), py * 2 + pz
        if m == 1:
            px, pz = lax.rem(x + r, 4), lax.rem(z + b, 2)
            return at(px, y, pz), px * 2 + pz
        px = lax.rem(x + r, 4)
        py = y + b * (1 - 2 * lax.rem(y, 2))
        return at(px, py, z), px * 2 + lax.rem(py, 2)

    def group4(m, k):
        if m == 0:
            px = lax.rem(x + k, 4)
            return at(px, y, z), px
        if m == 1:
            py = lax.rem(y + k, 4)
            return at(x, py, z), py
        py, pz = lax.rem(y + 2 * (k // 2), 4), lax.rem(z + k % 2, 2)
        return at(x, py, pz), (py // 2) * 2 + pz

    def remote(src, dst, ss, rs, device):
        return pltpu.make_async_remote_copy(
            src_ref=src, dst_ref=dst, send_sem=ss, recv_sem=rs, device_id=device, device_id_type=MESH
        )

    barrier = pltpu.get_barrier_semaphore()
    senders = [group8(0, k)[0] for k in range(1, 8)]
    senders += [group8(1, k)[0] for k in range(2, 8)]
    senders += [group8(2, k)[0] for k in (3, 5, 7)]
    senders += [sibling, across, prev_chip]
    for device in senders:
        pl.semaphore_signal(barrier, inc=1, device_id=device, device_id_type=MESH)

    my_cols = pl.ds(pl.multiple_of(c * DH, DH), DH)
    other_cols = pl.ds(pl.multiple_of(oc * DH, DH), DH)
    my_rows = pl.ds(pl.multiple_of(c * T, T), T)
    my_halo_rows = pl.ds(pl.multiple_of(WIN + c * T, WIN), T)

    def place(i, s):
        return (kb.at[s, my_halo_rows], vb.at[s, my_halo_rows], qb.at[s, my_rows])[i]

    inputs = (k_ref, v_ref, q_ref)

    def local_in(i, s):
        return pltpu.make_async_copy(inputs[i].at[s, :, my_cols], place(i, s), loc_sem.at[i, s])

    def to_sibling(i, s):
        return remote(
            inputs[i].at[s, :, other_cols], place(i, s), d2d_s.at[i, s], d2d_r.at[i, s], sibling
        )

    w_copies = [
        pltpu.make_async_copy(wg_ref.at[c], w.at[0], w_sem.at[0]),
        pltpu.make_async_copy(wu_ref.at[c], w.at[1], w_sem.at[1]),
        pltpu.make_async_copy(wd_ref.at[c], wdb, w_sem.at[2]),
    ]
    wo_copies = [
        pltpu.make_async_copy(wo_ref.at[:, pl.ds(i * 512, 512)], wo.at[i], wo_sem.at[i]) for i in range(2)
    ]
    local_in(0, 0).start()
    w_copies[0].start()
    w_copies[1].start()
    w_copies[2].start()
    local_in(1, 0).start()
    local_in(0, 1).start()
    local_in(1, 1).start()
    local_in(2, 0).start()
    local_in(2, 1).start()
    wo_copies[0].start()
    wo_copies[1].start()

    rate_send[...] = jnp.zeros_like(rate_send)
    for s in range(SEG):
        both = rate_ref[s]
        rates[c, s : s + 1, :] = jnp.where(c == 0, both[0:1], both[1:2])
        rate_send[s : s + 1, :] = jnp.where(c == 0, both[1:2], both[0:1])
    rate_copy = remote(rate_send, rates.at[c], rate_s, rate_r, sibling)

    w_copies[0].wait()
    wb[0] = w[0].astype(BF)
    w_copies[1].wait()
    wb[1] = w[1].astype(BF)
    w_copies[2].wait()
    w[2] = wdb[...].T
    wb[2] = w[2].astype(BF)

    def forward(s, half, j):
        start = pl.multiple_of(half * T + j * BLK, BLK)
        rows = pl.ds(pl.multiple_of(WIN + start, BLK), BLK)
        cols = pl.ds(start, BLK)
        key = kb[s, rows, :]
        value = vb[s, rows, :]
        rate = -rates[half, s : s + 1, pl.ds(pl.multiple_of(j * BLK, BLK), BLK)]
        g1 = nt(wb[0], key)
        g3 = nt(wb[1], key)
        back = nt(wb[2], value) * rate
        sg = sigmoid(g1)
        ga = g1 * sg
        act[:, cols] = (ga * g3 * rate).astype(BF)
        d1[:, cols] = (back * g3 * (sg + ga * (1.0 - sg))).astype(BF)
        d3[:, cols] = (back * ga).astype(BF)

    def rs(s, m, k):
        device, p = group8(m, k)
        return remote(gb.at[s, m, p], rsr.at[s, m, k - 1], rs_s.at[s, m, k - 1], rs_r.at[s, m, k - 1], device)

    def ar(s, m, k):
        mine = group4(m, 0)[1]
        ref = arb.at[s, m, mine]
        return remote(ref, ref, ar_s.at[s, m, k - 1], ar_r.at[s, m, k - 1], group4(m, k)[0])

    def ag(s, m, k):
        ref = gf.at[s, m, group8(m, 0)[1]]
        return remote(ref, ref, ag_s.at[s, m, k - 1], ag_r.at[s, m, k - 1], group8(m, k)[0])

    far_first = (5, 4, 3, 7, 2, 6, 1)
    order = (2, 0, 1)

    def gradients(s):
        keys = kb[s, pl.ds(WIN, TC), :]
        values = vb[s, pl.ds(WIN, TC), :]
        for m in order:
            grad = nn(act[...], values) if m == 2 else nn((d1, d3)[m][...], keys)
            for p in range(8):
                part = grad[p * 64 : (p + 1) * 64]
                g32[m, p] = part
                gb[s, m, p] = part.astype(BF)
            for k in far_first:
                rs(s, m, k).start()

    def reduce(s):
        for m in order:
            for k in far_first:
                rs(s, m, k).wait()
            total = g32[m, group8(m, 0)[1]]
            for k in range(1, 8):
                total = total + rsr[s, m, k - 1].astype(F32)
            arb[s, m, group4(m, 0)[1]] = total.astype(BF)
            for k in (2, 1, 3):
                ar(s, m, k).start()

    def spread(s):
        for m in order:
            for k in (1, 3, 2):
                ar(s, m, k).wait()
            total = arb[s, m, 0].astype(F32)
            for a in range(1, 4):
                total = total + arb[s, m, a].astype(F32)
            gf[s, m, group8(m, 0)[1]] = total.astype(BF)
            for k in far_first:
                ag(s, m, k).start()

    def update(s):
        for m in order:
            for k in far_first:
                ag(s, m, k).wait()
            rows = gf[s, m].reshape(FH, DH).astype(F32)
            norm = jnp.sqrt(jnp.sum(rows * rows, keepdims=True))
            xs[m] = rows * (1.0 / (norm + tiny))

        def single(_, carry):
            for m in order:
                cur = xs[m]
                low = cur.astype(BF)
                gram = tn(low, low)
                gram_b = gram.astype(BF)
                mixer = coef_b * gram + coef_c * nn(gram_b, gram_b)
                xs[m] = coef_a * cur + nn(low, mixer.astype(BF))
            return carry

        def double(_, carry):
            for m in order:
                cur = xs[m]
                hi, lo = split(cur)
                gram = tn(hi, hi) + (tn(hi, lo) + tn(lo, hi))
                gh, gl = split(gram)
                square = nn(gh, gh) + (nn(gh, gl) + nn(gl, gh))
                mh, ml = split(coef_b * gram + coef_c * square)
                xs[m] = coef_a * cur + (nn(hi, mh) + (nn(hi, ml) + nn(lo, mh)))
            return carry

        lax.fori_loop(0, SINGLE_STEPS, single, 0)
        lax.fori_loop(0, SPLIT_STEPS, double, 0)
        step = step_ref[c]
        for m in range(3):
            new = w[m] - step * xs[m]
            w[m] = new
            wb[m] = new.astype(BF)

    row_ids = lax.broadcasted_iota(jnp.int32, (BLK, 2 * BLK), 0)
    col_ids = lax.broadcasted_iota(jnp.int32, (BLK, 2 * BLK), 1)

    def attention(s, j):
        start = pl.multiple_of(j * BLK, BLK)
        query = qb[s, pl.ds(start, BLK), :]
        key = kb[s, pl.ds(start, 2 * BLK), :]
        value = vb[s, pl.ds(start, 2 * BLK), :]
        scores = nt(query, key) * (1.0 / 16.0)
        least = jnp.where(jnp.logical_and(chip == 0, j == 0), WIN, 0)
        allowed = (col_ids > row_ids) & (col_ids <= row_ids + WIN) & (col_ids >= least)
        scores = jnp.where(allowed, scores, -1e30)
        top = jnp.max(scores, axis=-1, keepdims=True)
        weights = jnp.exp(scores - top)
        total = jnp.sum(weights, axis=-1, keepdims=True)
        att[s, pl.ds(start, BLK), :] = nn(weights.astype(BF), value) / total

    def attend(s, first, last):
        def one(j, carry):
            attention(s, j)
            return carry

        lax.fori_loop(first, last, one, 0)

    def fast(s, half, j):
        start = pl.multiple_of(half * T + j * BLK, BLK)
        query = qb[s, pl.ds(start, BLK), :]
        g1 = nt(query, wb[0])
        g3 = nt(query, wb[1])
        hidden = (g1 * sigmoid(g1) * g3).astype(BF)
        return (att[s, pl.ds(start, BLK), :] + nn(hidden, wb[2])).astype(BF)

    def part(j):
        return pl.ds(j * BLK, BLK)

    def cs_copy(s, j):
        return remote(cs.at[s, part(j)], cb.at[s, c, part(j)], cs_s.at[s, j], cs_r.at[s, j], sibling)

    def z_copy(s, j):
        return remote(zs.at[s, part(j)], zr.at[s, part(j)], zs_s.at[s, j], zs_r.at[s, j], across)

    def project(s, j, group):
        return (
            nn(cb[s, 0, part(j)], wo[group, 0:DH, :]) + nn(cb[s, 1, part(j)], wo[group, DH : 2 * DH, :])
        ).astype(BF)

    def apply(s):
        for j in range(2):
            cs[s, part(j)] = fast(s, oc, j)
            cs_copy(s, j).start()
        for j in range(2):
            cb[s, c, part(j)] = fast(s, c, j)
            cs_copy(s, j).wait_recv()
            zs[s, part(j)] = project(s, j, 1 - hg)
            z_copy(s, j).start()
        for j in range(2):
            cs_copy(s, j).wait_send()
            zo[s, part(j)] = project(s, j, hg)

    def out_copy(s):
        return pltpu.make_async_copy(mx.at[s], mixed_ref.at[s], out_sem.at[s])

    def finish(s):
        for j in range(2):
            z_copy(s, j).wait()
            mx[s, part(j)] = (zo[s, part(j)].astype(F32) + zr[s, part(j)].astype(F32)).astype(BF)
        out_copy(s).start()

    local_in(0, 0).wait()
    local_in(1, 0).wait()
    forward(0, c, 0)
    pl.semaphore_wait(barrier, len(senders))
    to_sibling(0, 0).start()
    to_sibling(1, 0).start()
    rate_copy.start()
    for i, s in ((0, 1), (1, 1), (2, 0), (2, 1)):
        to_sibling(i, s).start()
    forward(0, c, 1)
    to_sibling(0, 0).wait()
    to_sibling(1, 0).wait()
    rate_copy.wait()
    forward(0, oc, 0)
    forward(0, oc, 1)
    gradients(0)

    def halo(i, s):
        buf = (kb, vb)[i]
        return remote(
            buf.at[s, pl.ds(TC, WIN)], buf.at[s, pl.ds(0, WIN)], halo_s.at[i, s], halo_r.at[i, s], next_chip
        )

    halo(0, 0).start()
    halo(1, 0).start()
    for i in range(3):
        local_in(i, 1).wait()
        to_sibling(i, 1).wait()
    local_in(2, 0).wait()
    to_sibling(2, 0).wait()
    halo(0, 1).start()
    halo(1, 1).start()
    for i in range(2):
        wo_copies[i].wait()

    reduce(0)
    halo(0, 0).wait()
    halo(1, 0).wait()
    attend(0, 0, 4)
    spread(0)
    halo(0, 1).wait()
    halo(1, 1).wait()
    attend(1, 0, 4)
    update(0)

    for j in range(2):
        forward(1, c, j)
        forward(1, oc, j)
    gradients(1)
    apply(0)
    reduce(1)
    spread(1)
    finish(0)
    update(1)
    apply(1)

    outs = (gate_ref.at[c], up_ref.at[c], down_ref.at[c])
    wdb[...] = w[2].T
    sources = (w.at[0], w.at[1], wdb)
    for m in range(3):
        remote(sources[m], outs[m], st_s.at[m], st_r.at[m], sibling).start()
        pltpu.make_async_copy(sources[m], outs[m], w_sem.at[m]).start()
    finish(1)
    for m in range(3):
        remote(sources[m], outs[m], st_s.at[m], st_r.at[m], sibling).wait()
        pltpu.make_async_copy(sources[m], outs[m], w_sem.at[m]).wait()
    for s in range(SEG):
        out_copy(s).wait()


def body(queries, keys, values, token_rate, step_size, w_gate, w_up, w_down, w_out):
    dma = pltpu.SemaphoreType.DMA
    anywhere = pl.BlockSpec(memory_space=pl.ANY)

    def b16(*shape):
        return pltpu.VMEM(shape, BF)

    def f32(*shape):
        return pltpu.VMEM(shape, F32)

    return pl.pallas_call(
        kernel,
        out_shape=(
            jax.ShapeDtypeStruct((SEG, T, 2 * DH), BF),
            jax.ShapeDtypeStruct((2, FH, DH), F32),
            jax.ShapeDtypeStruct((2, FH, DH), F32),
            jax.ShapeDtypeStruct((2, DH, FH), F32),
        ),
        in_specs=[
            anywhere, anywhere, anywhere,
            pl.BlockSpec(memory_space=pltpu.VMEM),
            pl.BlockSpec(memory_space=pltpu.SMEM),
            anywhere, anywhere, anywhere, anywhere,
        ],
        out_specs=(anywhere, anywhere, anywhere, anywhere),
        scratch_shapes=[
            b16(SEG, TC, DH), b16(SEG, WIN + TC, DH), b16(SEG, WIN + TC, DH),
            f32(2, 8, T), f32(8, T),
            f32(3, FH, DH), b16(3, FH, DH), f32(DH, FH), b16(2, 512, 512),
            b16(FH, TC), b16(FH, TC), b16(FH, TC),
            f32(3, 8, 64, DH), b16(SEG, 3, 8, 64, DH), b16(SEG, 3, 7, 64, DH), b16(SEG, 3, 4, 64, DH),
            b16(SEG, 3, 8, 64, DH), f32(3, FH, DH),
            f32(SEG, TC, DH), b16(SEG, T, DH), b16(SEG, 2, T, DH),
            b16(SEG, T, 512), b16(SEG, T, 512), b16(SEG, T, 512), b16(SEG, T, 512),
            dma((3, 2)), dma((3,)), dma((2,)), dma((3, 2)), dma((3, 2)), dma, dma, dma((2, 2)), dma((2, 2)),
            dma((2, 3, 7)), dma((2, 3, 7)), dma((2, 3, 3)), dma((2, 3, 3)), dma((2, 3, 7)), dma((2, 3, 7)),
            dma((2, 2)), dma((2, 2)), dma((2, 2)), dma((2, 2)), dma((3,)), dma((3,)), dma((2,)),
        ],
        compiler_params=pltpu.CompilerParams(
            collective_id=0, has_side_effects=True, vmem_limit_bytes=56 * 2**20
        ),
        name="layer",
    )(queries, keys, values, token_rate, step_size, w_gate, w_up, w_down, w_out)


def solution(mesh):
    return jax.shard_map(
        body,
        mesh=mesh,
        in_specs=(
            P(None, "seq", "head"),
            P(None, "seq", "head"),
            P(None, "seq", "head"),
            P(None, "head", "seq"),
            P("head"),
            P("head", None, None),
            P("head", None, None),
            P("head", None, None),
            P("head", None),
        ),
        out_specs=(
            P(None, "seq", "head"),
            P("head", None, None),
            P("head", None, None),
            P("head", None, None),
        ),
        check_vma=False,
    )
```

```python
import functools

import jax
import jax.numpy as jnp
from jax import lax
from jax.experimental import pallas as pl
from jax.experimental.pallas import tpu as pltpu
from jax.sharding import PartitionSpec as P

F32 = jnp.float32
BF = jnp.bfloat16
MESH = pl.DeviceIdType.MESH

DH = 256
FH = 512
WIN = 256
T = 512
TC = 2 * T
SEG = 2
BLK = 256
coef_a = 3.4445
coef_b = -4.775
coef_c = 2.0315
tiny = 1e-07

SINGLE_STEPS = 3
SPLIT_STEPS = 2

JOBS = ((2, 0, 2, 0, 0), (0, 0, 2, 1, 0), (1, 0, 1, 0, 1), (1, 8, 1, 1, 1))


def nn(a, b):
    return jnp.dot(a, b, preferred_element_type=F32)


def nt(a, b):
    return lax.dot_general(a, b, (((1,), (1,)), ((), ())), preferred_element_type=F32)


def tn(a, b):
    return lax.dot_general(a, b, (((0,), (0,)), ((), ())), preferred_element_type=F32)


def sigmoid(v):
    return 1.0 / (1.0 + jnp.exp(-v))


def split(a):
    high = a.astype(BF)
    return high, (a - high.astype(F32)).astype(BF)


def kernel(
    q_ref, k_ref, v_ref, rate_ref, step_ref, wg_ref, wu_ref, wd_ref, wo_ref,
    mixed_ref, gate_ref, up_ref, down_ref,
    qb, kb, vb, rates, rate_in, rate_send, w, wb, wdb, wo, act, d1, d3, g32, gb, rsr, arb, gf,
    att, cs, cb, zs, zo, zr, mx,
    loc_sem, w_sem, wo_sem, rate_l, d2d_s, d2d_r, rate_s, rate_r, halo_s, halo_r,
    rs_s, rs_r, ar_s, ar_r, ag_s, ag_r, cs_s, cs_r, zs_s, zs_r, st_s, st_r, out_sem,
):
    seq = lax.axis_index("seq")
    hg = lax.axis_index("head")
    c = lax.rem(seq, 2)
    z = lax.rem(seq // 2, 2)
    y = lax.rem(seq // 4, 4)
    x = seq // 16
    oc = 1 - c
    chip = seq // 2

    def at(px, py, pz, pc=None):
        return {"seq": ((px * 4 + py) * 2 + pz) * 2 + (c if pc is None else pc)}

    sibling = at(x, y, z, oc)
    across = {"head": 1 - hg}
    next_chip = {"seq": lax.rem(chip + 1, 32) * 2 + c}
    prev_chip = {"seq": lax.rem(chip + 31, 32) * 2 + c}

    def group8(job, k):
        _, _, _, line, shift = JOBS[job]
        r, b = k // 2, k % 2
        along, beside = (x, y) if line else (y, x)
        bit = lax.rem(beside + shift, 2)
        along = lax.rem(along + r, 4)
        beside = lax.rem(beside + b * (1 - 2 * bit) + 4, 4)
        px, py = (along, beside) if line else (beside, along)
        return at(px, py, z), along * 2 + lax.rem(bit + b, 2)

    def group4(job, k):
        _, _, _, line, shift = JOBS[job]
        beside, pz = lax.rem((y if line else x) + 2 * (k // 2), 4), lax.rem(z + k % 2, 2)
        index = (lax.rem(beside + shift, 4) // 2) * 2 + pz
        return (at(x, beside, pz) if line else at(beside, y, pz)), index

    def piece(job, p):
        _, first, rows, _, _ = JOBS[job]
        return pl.ds(first + p * rows, rows)

    def remote(src, dst, ss, rs, device):
        return pltpu.make_async_remote_copy(
            src_ref=src, dst_ref=dst, send_sem=ss, recv_sem=rs, device_id=device, device_id_type=MESH
        )

    barrier = pltpu.get_barrier_semaphore()
    offsets = [(i, j, 0) for i in range(4) for j in range(4) if (i, j) not in ((0, 0), (2, 2))]
    offsets += [(0, 0, 1), (0, 2, 1), (2, 0, 1)]
    senders = [at(lax.rem(x + i, 4), lax.rem(y + j, 4), lax.rem(z + k, 2)) for i, j, k in offsets]
    senders += [sibling, across, prev_chip]
    for device in senders:
        pl.semaphore_signal(barrier, inc=1, device_id=device, device_id_type=MESH)

    my_cols = pl.ds(pl.multiple_of(c * DH, DH), DH)
    other_cols = pl.ds(pl.multiple_of(oc * DH, DH), DH)
    my_rows = pl.ds(pl.multiple_of(c * T, T), T)
    my_halo_rows = pl.ds(pl.multiple_of(WIN + c * T, WIN), T)

    def place(i, s):
        return (kb.at[s, my_halo_rows], vb.at[s, my_halo_rows], qb.at[s, my_rows])[i]

    inputs = (k_ref, v_ref, q_ref)

    def local_in(i, s):
        return pltpu.make_async_copy(inputs[i].at[s, :, my_cols], place(i, s), loc_sem.at[i, s])

    def to_sibling(i, s):
        return remote(
            inputs[i].at[s, :, other_cols], place(i, s), d2d_s.at[i, s], d2d_r.at[i, s], sibling
        )

    w_copies = [
        pltpu.make_async_copy(wg_ref.at[c], w.at[0], w_sem.at[0]),
        pltpu.make_async_copy(wu_ref.at[c], w.at[1], w_sem.at[1]),
        pltpu.make_async_copy(wd_ref.at[c], wdb, w_sem.at[2]),
    ]
    wo_copies = [
        pltpu.make_async_copy(wo_ref.at[:, pl.ds(i * 512, 512)], wo.at[i], wo_sem.at[i]) for i in range(2)
    ]
    rate_load = pltpu.make_async_copy(rate_ref, rate_in, rate_l)
    rate_load.start()
    local_in(0, 0).start()
    w_copies[0].start()
    w_copies[1].start()
    w_copies[2].start()
    local_in(1, 0).start()
    local_in(0, 1).start()
    local_in(1, 1).start()
    local_in(2, 0).start()
    local_in(2, 1).start()
    wo_copies[0].start()
    wo_copies[1].start()

    rate_send[...] = jnp.zeros_like(rate_send)
    rate_load.wait()
    for s in range(SEG):
        both = rate_in[s]
        rates[c, s : s + 1, :] = jnp.where(c == 0, both[0:1], both[1:2])
        rate_send[s : s + 1, :] = jnp.where(c == 0, both[1:2], both[0:1])
    rate_copy = remote(rate_send, rates.at[c], rate_s, rate_r, sibling)

    w_copies[0].wait()
    wb[0] = w[0].astype(BF)
    w_copies[1].wait()
    wb[1] = w[1].astype(BF)
    def forward(s, half, j):
        start = pl.multiple_of(half * T + j * BLK, BLK)
        rows = pl.ds(pl.multiple_of(WIN + start, BLK), BLK)
        cols = pl.ds(start, BLK)
        key = kb[s, rows, :]
        value = vb[s, rows, :]
        rate = -rates[half, s : s + 1, pl.ds(pl.multiple_of(j * BLK, BLK), BLK)]
        g1 = nt(wb[0], key)
        g3 = nt(wb[1], key)
        back = nt(wb[2], value) * rate
        sg = sigmoid(g1)
        ga = g1 * sg
        act[:, cols] = (ga * g3 * rate).astype(BF)
        d1[:, cols] = (back * g3 * (sg + ga * (1.0 - sg))).astype(BF)
        d3[:, cols] = (back * ga).astype(BF)

    def rs(s, job, k):
        m, rows = JOBS[job][0], JOBS[job][2]
        device, p = group8(job, k)
        return remote(
            gb.at[s, m, piece(job, p)],
            rsr.at[s, job, k - 1, pl.ds(0, rows)],
            rs_s.at[s, job, k - 1],
            rs_r.at[s, job, k - 1],
            device,
        )

    def ar(s, job, k):
        ref = arb.at[s, job, group4(job, 0)[1], pl.ds(0, JOBS[job][2])]
        return remote(ref, ref, ar_s.at[s, job, k - 1], ar_r.at[s, job, k - 1], group4(job, k)[0])

    def ag(s, job, k):
        ref = gf.at[s, JOBS[job][0], piece(job, group8(job, 0)[1])]
        return remote(ref, ref, ag_s.at[s, job, k - 1], ag_r.at[s, job, k - 1], group8(job, k)[0])

    far_first = (5, 4, 3, 7, 2, 6, 1)
    order = (2, 0, 1)

    def gradients(s):
        keys = kb[s, pl.ds(WIN, TC), :]
        values = vb[s, pl.ds(WIN, TC), :]
        for m in order:
            grad = nn(act[...], values) if m == 2 else nn((d1, d3)[m][...], keys)
            grad = grad.reshape(16, 32, DH)
            g32[m] = grad
            gb[s, m] = grad.astype(BF)
            for k in far_first:
                for job in range(4):
                    if JOBS[job][0] == m:
                        rs(s, job, k).start()

    def reduce(s):
        for job in range(4):
            m, rows = JOBS[job][0], JOBS[job][2]
            for k in far_first:
                rs(s, job, k).wait()
            total = g32[m, piece(job, group8(job, 0)[1])]
            for k in range(1, 8):
                total = total + rsr[s, job, k - 1, 0:rows].astype(F32)
            arb[s, job, group4(job, 0)[1], 0:rows] = total.astype(BF)
            for k in (3, 2, 1):
                ar(s, job, k).start()

    def spread(s):
        for job in range(4):
            m, rows = JOBS[job][0], JOBS[job][2]
            for k in (1, 2, 3):
                ar(s, job, k).wait()
            total = arb[s, job, 0, 0:rows].astype(F32)
            for a in range(1, 4):
                total = total + arb[s, job, a, 0:rows].astype(F32)
            gf[s, m, piece(job, group8(job, 0)[1])] = total.astype(BF)
            for k in far_first:
                ag(s, job, k).start()

    def arrive(s):
        for job in range(4):
            for k in far_first:
                ag(s, job, k).wait()

    def update(s):
        cur = []
        for m in range(3):
            rows = gf[s, m].reshape(FH, DH).astype(F32)
            norm = jnp.sqrt(jnp.sum(rows * rows, keepdims=True))
            cur.append(rows * (1.0 / (norm + tiny)))
        for i in range(SINGLE_STEPS + SPLIT_STEPS):
            high = [a.astype(BF) for a in cur]
            gram = [tn(a, a) for a in high]
            if i < SINGLE_STEPS:
                gram_b = [a.astype(BF) for a in gram]
                square = [nn(a, a) for a in gram_b]
                mixer = [(coef_b * a + coef_c * b).astype(BF) for a, b in zip(gram, square)]
                change = [nn(a, b) for a, b in zip(high, mixer)]
            else:
                parts = [split(a) for a in gram]
                cross = [nn(a, b) for a, b in parts]
                square = [nn(a, a) + (b + b.T) for (a, _), b in zip(parts, cross)]
                mixer = [split(coef_b * a + coef_c * b) for a, b in zip(gram, square)]
                low = [(a - b.astype(F32)).astype(BF) for a, b in zip(cur, high)]
                change = [nn(a, b) + (nn(a, d) + nn(e, b)) for a, e, (b, d) in zip(high, low, mixer)]
            cur = [coef_a * a + b for a, b in zip(cur, change)]
        step = step_ref[c]
        for m in range(3):
            new = w[m] - step * cur[m]
            w[m] = new
            wb[m] = new.astype(BF)

    row_ids = lax.broadcasted_iota(jnp.int32, (BLK, 2 * BLK), 0)
    col_ids = lax.broadcasted_iota(jnp.int32, (BLK, 2 * BLK), 1)

    def attention(s, j):
        start = pl.multiple_of(j * BLK, BLK)
        query = qb[s, pl.ds(start, BLK), :]
        key = kb[s, pl.ds(start, 2 * BLK), :]
        value = vb[s, pl.ds(start, 2 * BLK), :]
        scores = nt(query, key) * (1.0 / 16.0)
        least = jnp.where(jnp.logical_and(chip == 0, j == 0), WIN, 0)
        allowed = (col_ids > row_ids) & (col_ids <= row_ids + WIN) & (col_ids >= least)
        scores = jnp.where(allowed, scores, -1e30)
        top = jnp.max(scores, axis=-1, keepdims=True)
        weights = jnp.exp(scores - top)
        total = jnp.sum(weights, axis=-1, keepdims=True)
        att[s, pl.ds(start, BLK), :] = nn(weights.astype(BF), value) / total

    def attend(s, first, last):
        def one(j, carry):
            attention(s, j)
            return carry

        lax.fori_loop(first, last, one, 0)

    def fast(s, half, j):
        start = pl.multiple_of(half * T + j * BLK, BLK)
        query = qb[s, pl.ds(start, BLK), :]
        g1 = nt(query, wb[0])
        g3 = nt(query, wb[1])
        hidden = (g1 * sigmoid(g1) * g3).astype(BF)
        return (att[s, pl.ds(start, BLK), :] + nn(hidden, wb[2])).astype(BF)

    def part(j):
        return pl.ds(j * BLK, BLK)

    def cs_copy(s, j):
        return remote(cs.at[s, part(j)], cb.at[s, c, part(j)], cs_s.at[s, j], cs_r.at[s, j], sibling)

    def z_copy(s, j):
        return remote(zs.at[s, part(j)], zr.at[s, part(j)], zs_s.at[s, j], zs_r.at[s, j], across)

    def project(s, j, group):
        return (
            nn(cb[s, 0, part(j)], wo[group, 0:DH, :]) + nn(cb[s, 1, part(j)], wo[group, DH : 2 * DH, :])
        ).astype(BF)

    def apply(s, send):
        for j in range(2):
            cs[s, part(j)] = fast(s, oc, j)
            cs_copy(s, j).start()
            cb[s, c, part(j)] = fast(s, c, j)
            cs_copy(s, j).wait_recv()
            zs[s, part(j)] = project(s, j, 1 - hg)
            if send:
                z_copy(s, j).start()
        for j in range(2):
            cs_copy(s, j).wait_send()
            zo[s, part(j)] = project(s, j, hg)

    def out_copy(s):
        return pltpu.make_async_copy(mx.at[s], mixed_ref.at[s], out_sem.at[s])

    def finish(s):
        for j in range(2):
            z_copy(s, j).wait()
            mx[s, part(j)] = (zo[s, part(j)].astype(F32) + zr[s, part(j)].astype(F32)).astype(BF)
        out_copy(s).start()

    def halo(i, s):
        buf = (kb, vb)[i]
        return remote(
            buf.at[s, pl.ds(TC, WIN)], buf.at[s, pl.ds(0, WIN)], halo_s.at[i, s], halo_r.at[i, s], next_chip
        )

    pl.semaphore_wait(barrier, len(senders))
    to_sibling(0, 0).start()
    to_sibling(1, 0).start()
    rate_copy.start()
    for i, s in ((0, 1), (1, 1), (2, 0), (2, 1)):
        to_sibling(i, s).start()
    w_copies[2].wait()
    w[2] = wdb[...].T
    wb[2] = w[2].astype(BF)
    local_in(0, 0).wait()
    local_in(1, 0).wait()
    forward(0, c, 0)
    forward(0, c, 1)
    to_sibling(0, 0).wait()
    to_sibling(1, 0).wait()
    rate_copy.wait()
    halo(0, 0).start()
    halo(1, 0).start()
    forward(0, oc, 0)
    forward(0, oc, 1)
    gradients(0)

    for i in range(3):
        local_in(i, 1).wait()
        to_sibling(i, 1).wait()
    local_in(2, 0).wait()
    to_sibling(2, 0).wait()
    for i in range(2):
        wo_copies[i].wait()

    reduce(0)
    halo(0, 0).wait()
    halo(1, 0).wait()
    attend(0, 0, 4)
    spread(0)
    attend(1, 1, 4)
    arrive(0)
    halo(0, 1).start()
    halo(1, 1).start()
    update(0)

    for j in range(2):
        forward(1, c, j)
        forward(1, oc, j)
    gradients(1)
    apply(0, False)
    reduce(1)
    halo(0, 1).wait()
    halo(1, 1).wait()
    attend(1, 0, 1)
    spread(1)
    for j in range(2):
        z_copy(0, j).start()
    arrive(1)
    update(1)
    apply(1, True)

    outs = (gate_ref.at[c], up_ref.at[c], down_ref.at[c])
    wdb[...] = w[2].T
    sources = (w.at[0], w.at[1], wdb)
    for m in range(3):
        remote(sources[m], outs[m], st_s.at[m], st_r.at[m], sibling).start()
        pltpu.make_async_copy(sources[m], outs[m], w_sem.at[m]).start()
    finish(0)
    finish(1)
    for m in range(3):
        remote(sources[m], outs[m], st_s.at[m], st_r.at[m], sibling).wait()
        pltpu.make_async_copy(sources[m], outs[m], w_sem.at[m]).wait()
    for s in range(SEG):
        out_copy(s).wait()


def deliver(*refs):
    ins, outs, bufs, get_sem, put_sem = refs[0:4], refs[4:8], refs[8:12], refs[12], refs[13]
    gets, puts = [], []
    for i in (1, 2, 3, 0):
        for h in range(2):
            gets.append(pltpu.make_async_copy(ins[i].at[h], bufs[i].at[h], get_sem.at[i, h]))
            puts.append(pltpu.make_async_copy(bufs[i].at[h], outs[i].at[h], put_sem.at[i, h]))
    for get in gets:
        get.start()
    for get, put in zip(gets, puts):
        get.wait()
        put.start()
    for put in puts:
        put.wait()


def body(queries, keys, values, token_rate, step_size, w_gate, w_up, w_down, w_out):
    dma = pltpu.SemaphoreType.DMA
    anywhere = pl.BlockSpec(memory_space=pl.ANY)

    def b16(*shape):
        return pltpu.VMEM(shape, BF)

    def f32(*shape):
        return pltpu.VMEM(shape, F32)

    results = pl.pallas_call(
        kernel,
        out_shape=(
            jax.ShapeDtypeStruct((SEG, T, 2 * DH), BF),
            jax.ShapeDtypeStruct((2, FH, DH), F32),
            jax.ShapeDtypeStruct((2, FH, DH), F32),
            jax.ShapeDtypeStruct((2, DH, FH), F32),
        ),
        in_specs=[
            anywhere, anywhere, anywhere,
            anywhere,
            pl.BlockSpec(memory_space=pltpu.SMEM),
            anywhere, anywhere, anywhere, anywhere,
        ],
        out_specs=(anywhere, anywhere, anywhere, anywhere),
        scratch_shapes=[
            b16(SEG, TC, DH), b16(SEG, WIN + TC, DH), b16(SEG, WIN + TC, DH),
            f32(2, 8, T), f32(SEG, 2, T), f32(8, T),
            f32(3, FH, DH), b16(3, FH, DH), f32(DH, FH), b16(2, 512, 512),
            b16(FH, TC), b16(FH, TC), b16(FH, TC),
            f32(3, 16, 32, DH), b16(SEG, 3, 16, 32, DH), b16(SEG, 4, 7, 2, 32, DH), b16(SEG, 4, 4, 2, 32, DH),
            b16(SEG, 3, 16, 32, DH),
            f32(SEG, TC, DH), b16(SEG, T, DH), b16(SEG, 2, T, DH),
            b16(SEG, T, 512), b16(SEG, T, 512), b16(SEG, T, 512), b16(SEG, T, 512),
            dma((3, 2)), dma((3,)), dma((2,)), dma, dma((3, 2)), dma((3, 2)), dma, dma, dma((2, 2)), dma((2, 2)),
            dma((2, 4, 7)), dma((2, 4, 7)), dma((2, 4, 3)), dma((2, 4, 3)), dma((2, 4, 7)), dma((2, 4, 7)),
            dma((2, 2)), dma((2, 2)), dma((2, 2)), dma((2, 2)), dma((3,)), dma((3,)), dma((2,)),
        ],
        compiler_params=pltpu.CompilerParams(
            collective_id=0, has_side_effects=True, vmem_limit_bytes=56 * 2**20
        ),
        name="layer",
    )(queries, keys, values, token_rate, step_size, w_gate, w_up, w_down, w_out)
    return pl.pallas_call(
        deliver,
        out_shape=tuple(jax.ShapeDtypeStruct(a.shape, a.dtype) for a in results),
        in_specs=[anywhere] * 4,
        out_specs=(anywhere,) * 4,
        scratch_shapes=[pltpu.VMEM(a.shape, a.dtype) for a in results] + [dma((4, 2)), dma((4, 2))],
        compiler_params=pltpu.CompilerParams(vmem_limit_bytes=16 * 2**20),
        name="deliver",
    )(*results)


def solution(mesh):
    return jax.shard_map(
        body,
        mesh=mesh,
        in_specs=(
            P(None, "seq", "head"),
            P(None, "seq", "head"),
            P(None, "seq", "head"),
            P(None, "head", "seq"),
            P("head"),
            P("head", None, None),
            P("head", None, None),
            P("head", None, None),
            P("head", None),
        ),
        out_specs=(
            P(None, "seq", "head"),
            P("head", None, None),
            P("head", None, None),
            P("head", None, None),
        ),
        check_vma=False,
    )
```

```python
import functools

import jax
import jax.numpy as jnp
from jax import lax
from jax.experimental import pallas as pl
from jax.experimental.pallas import tpu as pltpu
from jax.sharding import PartitionSpec as P

F32 = jnp.float32
BF = jnp.bfloat16
MESH = pl.DeviceIdType.MESH

DH = 256
FH = 512
WIN = 256
T = 512
TC = 2 * T
SEG = 2
BLK = 256
ROWS = (256, 128)
coef_a = 3.4445
coef_b = -4.775
coef_c = 2.0315
tiny = 1e-07

SINGLE_STEPS = 3
SPLIT_STEPS = 2

JOBS = ((2, 0, 2, 0, 0), (0, 0, 2, 1, 0), (1, 0, 1, 0, 1), (1, 8, 1, 1, 1))


def nn(a, b):
    return jnp.dot(a, b, preferred_element_type=F32)


def nt(a, b):
    return lax.dot_general(a, b, (((1,), (1,)), ((), ())), preferred_element_type=F32)


def tn(a, b):
    return lax.dot_general(a, b, (((0,), (0,)), ((), ())), preferred_element_type=F32)


def sigmoid(v):
    return 1.0 / (1.0 + jnp.exp(-v))


def split(a):
    high = a.astype(BF)
    return high, (a - high.astype(F32)).astype(BF)


def kernel(
    q_ref, k_ref, v_ref, rate_ref, step_ref, wg_ref, wu_ref, wd_ref, wo_ref,
    mixed_ref, gate_ref, up_ref, down_ref,
    qb, kb, vb, rates, rate_in, rate_send, w, wb, wdb, wo, act, d1, d3, g32, gb, rsr, arb, gf,
    att, cs, cb, zs, zo, zr, mx,
    loc_sem, w_sem, wo_sem, rate_l, d2d_s, d2d_r, rate_s, rate_r, halo_s, halo_r,
    rs_s, rs_r, ar_s, ar_r, ag_s, ag_r, cs_s, cs_r, zs_s, zs_r, st_s, st_r, out_sem,
):
    seq = lax.axis_index("seq")
    hg = lax.axis_index("head")
    c = lax.rem(seq, 2)
    z = lax.rem(seq // 2, 2)
    y = lax.rem(seq // 4, 4)
    x = seq // 16
    oc = 1 - c
    chip = seq // 2

    def at(px, py, pz, pc=None):
        return {"seq": ((px * 4 + py) * 2 + pz) * 2 + (c if pc is None else pc)}

    sibling = at(x, y, z, oc)
    across = {"head": 1 - hg}
    next_chip = {"seq": lax.rem(chip + 1, 32) * 2 + c}
    prev_chip = {"seq": lax.rem(chip + 31, 32) * 2 + c}

    def group8(job, k):
        _, _, _, line, shift = JOBS[job]
        r, b = k // 2, k % 2
        along, beside = (x, y) if line else (y, x)
        bit = lax.rem(beside + shift, 2)
        along = lax.rem(along + r, 4)
        beside = lax.rem(beside + b * (1 - 2 * bit) + 4, 4)
        px, py = (along, beside) if line else (beside, along)
        return at(px, py, z), along * 2 + lax.rem(bit + b, 2)

    def group4(job, k):
        _, _, _, line, shift = JOBS[job]
        beside, pz = lax.rem((y if line else x) + 2 * (k // 2), 4), lax.rem(z + k % 2, 2)
        index = (lax.rem(beside + shift, 4) // 2) * 2 + pz
        return (at(x, beside, pz) if line else at(beside, y, pz)), index

    def piece(job, p):
        _, first, rows, _, _ = JOBS[job]
        return pl.ds(first + p * rows, rows)

    def remote(src, dst, ss, rs, device):
        return pltpu.make_async_remote_copy(
            src_ref=src, dst_ref=dst, send_sem=ss, recv_sem=rs, device_id=device, device_id_type=MESH
        )

    barrier = pltpu.get_barrier_semaphore()
    offsets = [(i, j, 0) for i in range(4) for j in range(4) if (i, j) not in ((0, 0), (2, 2))]
    offsets += [(0, 0, 1), (0, 2, 1), (2, 0, 1)]
    senders = [at(lax.rem(x + i, 4), lax.rem(y + j, 4), lax.rem(z + k, 2)) for i, j, k in offsets]
    senders += [sibling, across, prev_chip]
    for device in senders:
        pl.semaphore_signal(barrier, inc=1, device_id=device, device_id_type=MESH)

    my_cols = pl.ds(pl.multiple_of(c * DH, DH), DH)
    other_cols = pl.ds(pl.multiple_of(oc * DH, DH), DH)
    my_rows = pl.ds(pl.multiple_of(c * T, T), T)
    my_halo_rows = pl.ds(pl.multiple_of(WIN + c * T, WIN), T)

    def place(i, s):
        return (kb.at[s, my_halo_rows], vb.at[s, my_halo_rows], qb.at[s, my_rows])[i]

    inputs = (k_ref, v_ref, q_ref)

    def local_in(i, s):
        return pltpu.make_async_copy(inputs[i].at[s, :, my_cols], place(i, s), loc_sem.at[i, s])

    def to_sibling(i, s):
        return remote(
            inputs[i].at[s, :, other_cols], place(i, s), d2d_s.at[i, s], d2d_r.at[i, s], sibling
        )

    w_copies = [
        pltpu.make_async_copy(wg_ref.at[c], w.at[0], w_sem.at[0]),
        pltpu.make_async_copy(wu_ref.at[c], w.at[1], w_sem.at[1]),
        pltpu.make_async_copy(wd_ref.at[c], wdb, w_sem.at[2]),
    ]
    wo_copies = [
        pltpu.make_async_copy(wo_ref.at[:, pl.ds(i * 512, 512)], wo.at[i], wo_sem.at[i]) for i in range(2)
    ]
    rate_load = pltpu.make_async_copy(rate_ref, rate_in, rate_l)
    rate_load.start()
    local_in(0, 0).start()
    w_copies[0].start()
    w_copies[1].start()
    w_copies[2].start()
    local_in(1, 0).start()
    local_in(0, 1).start()
    local_in(1, 1).start()
    local_in(2, 0).start()
    local_in(2, 1).start()
    wo_copies[0].start()
    wo_copies[1].start()

    rate_send[...] = jnp.zeros_like(rate_send)
    rate_load.wait()
    for s in range(SEG):
        both = rate_in[s]
        rates[c, s : s + 1, :] = jnp.where(c == 0, both[0:1], both[1:2])
        rate_send[s : s + 1, :] = jnp.where(c == 0, both[1:2], both[0:1])
    rate_copy = remote(rate_send, rates.at[c], rate_s, rate_r, sibling)

    w_copies[0].wait()
    wb[0] = w[0].astype(BF)
    w_copies[1].wait()
    wb[1] = w[1].astype(BF)
    def forward(s, half, j):
        start = pl.multiple_of(half * T + j * BLK, BLK)
        rows = pl.ds(pl.multiple_of(WIN + start, BLK), BLK)
        cols = pl.ds(start, BLK)
        key = kb[s, rows, :]
        value = vb[s, rows, :]
        rate = -rates[half, s : s + 1, pl.ds(pl.multiple_of(j * BLK, BLK), BLK)]
        g1 = nt(wb[0], key)
        g3 = nt(wb[1], key)
        back = nt(wb[2], value) * rate
        sg = sigmoid(g1)
        ga = g1 * sg
        act[:, cols] = (ga * g3 * rate).astype(BF)
        d1[:, cols] = (back * g3 * (sg + ga * (1.0 - sg))).astype(BF)
        d3[:, cols] = (back * ga).astype(BF)

    def rs(s, job, k):
        m, rows = JOBS[job][0], JOBS[job][2]
        device, p = group8(job, k)
        return remote(
            gb.at[s, m, piece(job, p)],
            rsr.at[s, job, k - 1, pl.ds(0, rows)],
            rs_s.at[s, job, k - 1],
            rs_r.at[s, job, k - 1],
            device,
        )

    def ar(s, job, k):
        ref = arb.at[s, job, group4(job, 0)[1], pl.ds(0, JOBS[job][2])]
        return remote(ref, ref, ar_s.at[s, job, k - 1], ar_r.at[s, job, k - 1], group4(job, k)[0])

    def ag(s, job, k):
        ref = gf.at[s, JOBS[job][0], piece(job, group8(job, 0)[1])]
        return remote(ref, ref, ag_s.at[s, job, k - 1], ag_r.at[s, job, k - 1], group8(job, k)[0])

    far_first = (5, 4, 3, 7, 2, 6, 1)
    order = (2, 0, 1)

    def gradients(s):
        keys = kb[s, pl.ds(WIN, TC), :]
        values = vb[s, pl.ds(WIN, TC), :]
        for m in order:
            grad = nn(act[...], values) if m == 2 else nn((d1, d3)[m][...], keys)
            grad = grad.reshape(16, 32, DH)
            g32[m] = grad
            gb[s, m] = grad.astype(BF)
            for k in far_first:
                for job in range(4):
                    if JOBS[job][0] == m:
                        rs(s, job, k).start()

    def reduce(s):
        for job in range(4):
            m, rows = JOBS[job][0], JOBS[job][2]
            for k in far_first:
                rs(s, job, k).wait()
            total = g32[m, piece(job, group8(job, 0)[1])]
            for k in range(1, 8):
                total = total + rsr[s, job, k - 1, 0:rows].astype(F32)
            arb[s, job, group4(job, 0)[1], 0:rows] = total.astype(BF)
            for k in (3, 2, 1):
                ar(s, job, k).start()

    def spread(s):
        for job in range(4):
            m, rows = JOBS[job][0], JOBS[job][2]
            for k in (1, 2, 3):
                ar(s, job, k).wait()
            total = arb[s, job, 0, 0:rows].astype(F32)
            for a in range(1, 4):
                total = total + arb[s, job, a, 0:rows].astype(F32)
            gf[s, m, piece(job, group8(job, 0)[1])] = total.astype(BF)
            for k in far_first:
                ag(s, job, k).start()

    def arrive(s):
        for job in range(4):
            for k in far_first:
                ag(s, job, k).wait()

    def update(s):
        cur = []
        for m in range(3):
            rows = gf[s, m].reshape(FH, DH).astype(F32)
            norm = jnp.sqrt(jnp.sum(rows * rows, keepdims=True))
            cur.append(rows * (1.0 / (norm + tiny)))
        for i in range(SINGLE_STEPS + SPLIT_STEPS):
            high = [a.astype(BF) for a in cur]
            gram = [tn(a, a) for a in high]
            if i < SINGLE_STEPS:
                gram_b = [a.astype(BF) for a in gram]
                square = [nn(a, a) for a in gram_b]
                mixer = [(coef_b * a + coef_c * b).astype(BF) for a, b in zip(gram, square)]
                change = [nn(a, b) for a, b in zip(high, mixer)]
            else:
                parts = [split(a) for a in gram]
                cross = [nn(a, b) for a, b in parts]
                square = [nn(a, a) + (b + b.T) for (a, _), b in zip(parts, cross)]
                mixer = [split(coef_b * a + coef_c * b) for a, b in zip(gram, square)]
                low = [(a - b.astype(F32)).astype(BF) for a, b in zip(cur, high)]
                change = [nn(a, b) + (nn(a, d) + nn(e, b)) for a, e, (b, d) in zip(high, low, mixer)]
            cur = [coef_a * a + b for a, b in zip(cur, change)]
        step = step_ref[c]
        for m in range(3):
            new = w[m] - step * cur[m]
            w[m] = new
            wb[m] = new.astype(BF)

    row_ids = lax.broadcasted_iota(jnp.int32, (BLK, 2 * BLK), 0)
    col_ids = lax.broadcasted_iota(jnp.int32, (BLK, 2 * BLK), 1)

    def attention(s, j):
        start = pl.multiple_of(j * BLK, BLK)
        query = qb[s, pl.ds(start, BLK), :]
        key = kb[s, pl.ds(start, 2 * BLK), :]
        value = vb[s, pl.ds(start, 2 * BLK), :]
        scores = nt(query, key) * (1.0 / 16.0)
        least = jnp.where(jnp.logical_and(chip == 0, j == 0), WIN, 0)
        allowed = (col_ids > row_ids) & (col_ids <= row_ids + WIN) & (col_ids >= least)
        scores = jnp.where(allowed, scores, -1e30)
        top = jnp.max(scores, axis=-1, keepdims=True)
        weights = jnp.exp(scores - top)
        total = jnp.sum(weights, axis=-1, keepdims=True)
        att[s, pl.ds(start, BLK), :] = nn(weights.astype(BF), value) / total

    def attend(s, first, last):
        def one(j, carry):
            attention(s, j)
            return carry

        lax.fori_loop(first, last, one, 0)

    def fast(s, half, rows):
        start = pl.multiple_of(half * T + rows.start, rows.size)
        query = qb[s, pl.ds(start, rows.size), :]
        g1 = nt(query, wb[0])
        g3 = nt(query, wb[1])
        hidden = (g1 * sigmoid(g1) * g3).astype(BF)
        return (att[s, pl.ds(start, rows.size), :] + nn(hidden, wb[2])).astype(BF)

    def part(s, j):
        return pl.ds(j * ROWS[s], ROWS[s])

    def cs_copy(s, j):
        rows = part(s, j)
        return remote(cs.at[s, rows], cb.at[s, c, rows], cs_s.at[s, j], cs_r.at[s, j], sibling)

    def z_copy(s, j):
        rows = part(s, j)
        return remote(zs.at[s, rows], zr.at[s, rows], zs_s.at[s, j], zs_r.at[s, j], across)

    def project(s, j, group):
        rows = part(s, j)
        return (
            nn(cb[s, 0, rows], wo[group, 0:DH, :]) + nn(cb[s, 1, rows], wo[group, DH : 2 * DH, :])
        ).astype(BF)

    def apply(s):
        count = T // ROWS[s]
        for j in range(count):
            cs[s, part(s, j)] = fast(s, oc, part(s, j))
            cs_copy(s, j).start()
            cb[s, c, part(s, j)] = fast(s, c, part(s, j))
            cs_copy(s, j).wait_recv()
            zs[s, part(s, j)] = project(s, j, 1 - hg)
            z_copy(s, j).start()
        for j in range(count):
            cs_copy(s, j).wait_send()
            zo[s, part(s, j)] = project(s, j, hg)

    def out_copy(s, j):
        rows = part(s, j)
        return pltpu.make_async_copy(mx.at[s, rows], mixed_ref.at[s, rows], out_sem.at[s, j])

    def finish(s):
        for j in range(T // ROWS[s]):
            rows = part(s, j)
            z_copy(s, j).wait()
            mx[s, rows] = (zo[s, rows].astype(F32) + zr[s, rows].astype(F32)).astype(BF)
            out_copy(s, j).start()

    def halo(i, s):
        buf = (kb, vb)[i]
        return remote(
            buf.at[s, pl.ds(TC, WIN)], buf.at[s, pl.ds(0, WIN)], halo_s.at[i, s], halo_r.at[i, s], next_chip
        )

    pl.semaphore_wait(barrier, len(senders))
    to_sibling(0, 0).start()
    to_sibling(1, 0).start()
    rate_copy.start()
    for i, s in ((0, 1), (1, 1), (2, 0), (2, 1)):
        to_sibling(i, s).start()
    w_copies[2].wait()
    w[2] = wdb[...].T
    wb[2] = w[2].astype(BF)
    local_in(0, 0).wait()
    local_in(1, 0).wait()
    forward(0, c, 0)
    forward(0, c, 1)
    to_sibling(0, 0).wait()
    to_sibling(1, 0).wait()
    rate_copy.wait()
    forward(0, oc, 0)
    forward(0, oc, 1)
    gradients(0)

    for i in range(3):
        local_in(i, 1).wait()
        to_sibling(i, 1).wait()
    local_in(2, 0).wait()
    to_sibling(2, 0).wait()
    for i in range(2):
        wo_copies[i].wait()

    reduce(0)
    attend(0, 1, 4)
    spread(0)
    arrive(0)
    halos = [halo(i, s) for s in range(SEG) for i in range(2)]
    for copy in halos:
        copy.start()
    update(0)

    for j in range(2):
        forward(1, c, j)
        forward(1, oc, j)
    gradients(1)
    attend(1, 1, 4)
    reduce(1)
    for copy in halos:
        copy.wait()
    attend(0, 0, 1)
    attend(1, 0, 1)
    spread(1)
    apply(0)
    arrive(1)
    update(1)
    apply(1)

    outs = (gate_ref.at[c], up_ref.at[c], down_ref.at[c])
    wdb[...] = w[2].T
    sources = (w.at[0], w.at[1], wdb)
    for m in range(3):
        remote(sources[m], outs[m], st_s.at[m], st_r.at[m], sibling).start()
        pltpu.make_async_copy(sources[m], outs[m], w_sem.at[m]).start()
    finish(0)
    finish(1)
    for m in range(3):
        remote(sources[m], outs[m], st_s.at[m], st_r.at[m], sibling).wait()
        pltpu.make_async_copy(sources[m], outs[m], w_sem.at[m]).wait()
    for s in range(SEG):
        for j in range(T // ROWS[s]):
            out_copy(s, j).wait()


def deliver(*refs):
    ins, outs, bufs, get_sem, put_sem = refs[0:4], refs[4:8], refs[8:12], refs[12], refs[13]
    gets, puts = [], []
    for i in (1, 2, 3, 0):
        for h in range(2):
            gets.append(pltpu.make_async_copy(ins[i].at[h], bufs[i].at[h], get_sem.at[i, h]))
            puts.append(pltpu.make_async_copy(bufs[i].at[h], outs[i].at[h], put_sem.at[i, h]))
    for get in gets:
        get.start()
    for get, put in zip(gets, puts):
        get.wait()
        put.start()
    for put in puts:
        put.wait()


def body(queries, keys, values, token_rate, step_size, w_gate, w_up, w_down, w_out):
    dma = pltpu.SemaphoreType.DMA
    anywhere = pl.BlockSpec(memory_space=pl.ANY)

    def b16(*shape):
        return pltpu.VMEM(shape, BF)

    def f32(*shape):
        return pltpu.VMEM(shape, F32)

    results = pl.pallas_call(
        kernel,
        out_shape=(
            jax.ShapeDtypeStruct((SEG, T, 2 * DH), BF),
            jax.ShapeDtypeStruct((2, FH, DH), F32),
            jax.ShapeDtypeStruct((2, FH, DH), F32),
            jax.ShapeDtypeStruct((2, DH, FH), F32),
        ),
        in_specs=[
            anywhere, anywhere, anywhere,
            anywhere,
            pl.BlockSpec(memory_space=pltpu.SMEM),
            anywhere, anywhere, anywhere, anywhere,
        ],
        out_specs=(anywhere, anywhere, anywhere, anywhere),
        scratch_shapes=[
            b16(SEG, TC, DH), b16(SEG, WIN + TC, DH), b16(SEG, WIN + TC, DH),
            f32(2, 8, T), f32(SEG, 2, T), f32(8, T),
            f32(3, FH, DH), b16(3, FH, DH), f32(DH, FH), b16(2, 512, 512),
            b16(FH, TC), b16(FH, TC), b16(FH, TC),
            f32(3, 16, 32, DH), b16(SEG, 3, 16, 32, DH), b16(SEG, 4, 7, 2, 32, DH), b16(SEG, 4, 4, 2, 32, DH),
            b16(SEG, 3, 16, 32, DH),
            f32(SEG, TC, DH), b16(SEG, T, DH), b16(SEG, 2, T, DH),
            b16(SEG, T, 512), b16(SEG, T, 512), b16(SEG, T, 512), b16(SEG, T, 512),
            dma((3, 2)), dma((3,)), dma((2,)), dma, dma((3, 2)), dma((3, 2)), dma, dma, dma((2, 2)), dma((2, 2)),
            dma((2, 4, 7)), dma((2, 4, 7)), dma((2, 4, 3)), dma((2, 4, 3)), dma((2, 4, 7)), dma((2, 4, 7)),
            dma((2, 4)), dma((2, 4)), dma((2, 4)), dma((2, 4)), dma((3,)), dma((3,)), dma((2, 4)),
        ],
        compiler_params=pltpu.CompilerParams(
            collective_id=0, has_side_effects=True, vmem_limit_bytes=56 * 2**20
        ),
        name="layer",
    )(queries, keys, values, token_rate, step_size, w_gate, w_up, w_down, w_out)
    return pl.pallas_call(
        deliver,
        out_shape=tuple(jax.ShapeDtypeStruct(a.shape, a.dtype) for a in results),
        in_specs=[anywhere] * 4,
        out_specs=(anywhere,) * 4,
        scratch_shapes=[pltpu.VMEM(a.shape, a.dtype) for a in results] + [dma((4, 2)), dma((4, 2))],
        compiler_params=pltpu.CompilerParams(vmem_limit_bytes=60 * 2**20),
        name="deliver",
    )(*results)


def solution(mesh):
    return jax.shard_map(
        body,
        mesh=mesh,
        in_specs=(
            P(None, "seq", "head"),
            P(None, "seq", "head"),
            P(None, "seq", "head"),
            P(None, "head", "seq"),
            P("head"),
            P("head", None, None),
            P("head", None, None),
            P("head", None, None),
            P("head", None),
        ),
        out_specs=(
            P(None, "seq", "head"),
            P("head", None, None),
            P("head", None, None),
            P("head", None, None),
        ),
        check_vma=False,
    )
```

```python
import functools

import jax
import jax.numpy as jnp
from jax import lax
from jax.experimental import pallas as pl
from jax.experimental.pallas import tpu as pltpu
from jax.sharding import PartitionSpec as P

F32 = jnp.float32
BF = jnp.bfloat16
MESH = pl.DeviceIdType.MESH

DH = 256
FH = 512
WIN = 256
T = 512
TC = 2 * T
SEG = 2
BLK = 256
ROWS = (256, 128)
coef_a = 3.4445
coef_b = -4.775
coef_c = 2.0315
tiny = 1e-07

SINGLE_STEPS = 3
SPLIT_STEPS = 2

JOBS = ((2, 0, 2, 2, 0), (0, 0, 2, 3, 0), (1, 0, 1, 0, 0), (1, 8, 1, 1, 0))


def nn(a, b):
    return jnp.dot(a, b, preferred_element_type=F32)


def nt(a, b):
    return lax.dot_general(a, b, (((1,), (1,)), ((), ())), preferred_element_type=F32)


def tn(a, b):
    return lax.dot_general(a, b, (((0,), (0,)), ((), ())), preferred_element_type=F32)


def sigmoid(v):
    return 1.0 / (1.0 + jnp.exp(-v))


def split(a):
    high = a.astype(BF)
    return high, (a - high.astype(F32)).astype(BF)


def kernel(
    q_ref, k_ref, v_ref, rate_ref, step_ref, wg_ref, wu_ref, wd_ref, wo_ref,
    mixed_ref, gate_ref, up_ref, down_ref,
    qb, kb, vb, rates, rate_in, rate_send, w, wb, wdb, wo, act, d1, d3, g32, gb, rsr, arb, gf,
    att, cs, cb, zs, zo, zr, mx,
    loc_sem, w_sem, wo_sem, rate_l, d2d_s, d2d_r, rate_s, rate_r, halo_s, halo_r,
    rs_s, rs_r, ar_s, ar_r, ag_s, ag_r, cs_s, cs_r, zs_s, zs_r, st_s, st_r, out_sem,
):
    seq = lax.axis_index("seq")
    hg = lax.axis_index("head")
    c = lax.rem(seq, 2)
    z = lax.rem(seq // 2, 2)
    y = lax.rem(seq // 4, 4)
    x = seq // 16
    oc = 1 - c
    chip = seq // 2

    def at(px, py, pz, pc=None):
        return {"seq": ((px * 4 + py) * 2 + pz) * 2 + (c if pc is None else pc)}

    sibling = at(x, y, z, oc)
    across = {"head": 1 - hg}
    next_chip = {"seq": lax.rem(chip + 1, 32) * 2 + c}
    prev_chip = {"seq": lax.rem(chip + 31, 32) * 2 + c}

    def group8(job, k):
        _, _, _, line, shift = JOBS[job]
        r, b = k // 2, k % 2
        if line > 1:
            along, pz = lax.rem((x if line == 3 else y) + r, 4), lax.rem(z + b, 2)
            return (at(along, y, pz) if line == 3 else at(x, along, pz)), along * 2 + pz
        along, beside = (x, y) if line else (y, x)
        bit = lax.rem(beside + shift, 2)
        along = lax.rem(along + r, 4)
        beside = lax.rem(beside + b * (1 - 2 * bit) + 4, 4)
        px, py = (along, beside) if line else (beside, along)
        return at(px, py, z), along * 2 + lax.rem(bit + b, 2)

    def group4(job, k):
        _, _, _, line, shift = JOBS[job]
        if line > 1:
            across_line = lax.rem((y if line == 3 else x) + k, 4)
            return (at(x, across_line, z) if line == 3 else at(across_line, y, z)), across_line
        beside, pz = lax.rem((y if line else x) + 2 * (k // 2), 4), lax.rem(z + k % 2, 2)
        index = (lax.rem(beside + shift, 4) // 2) * 2 + pz
        return (at(x, beside, pz) if line else at(beside, y, pz)), index

    def piece(job, p):
        _, first, rows, _, _ = JOBS[job]
        return pl.ds(first + p * rows, rows)

    def remote(src, dst, ss, rs, device):
        return pltpu.make_async_remote_copy(
            src_ref=src, dst_ref=dst, send_sem=ss, recv_sem=rs, device_id=device, device_id_type=MESH
        )

    barrier = pltpu.get_barrier_semaphore()
    offsets = [(i, j, 0) for i in range(4) for j in range(4) if (i, j) not in ((0, 0), (2, 2))]
    offsets += [(0, j, 1) for j in range(4)] + [(i, 0, 1) for i in range(1, 4)]
    senders = [at(lax.rem(x + i, 4), lax.rem(y + j, 4), lax.rem(z + k, 2)) for i, j, k in offsets]
    senders += [sibling, across, prev_chip]
    for device in senders:
        pl.semaphore_signal(barrier, inc=1, device_id=device, device_id_type=MESH)

    my_cols = pl.ds(pl.multiple_of(c * DH, DH), DH)
    other_cols = pl.ds(pl.multiple_of(oc * DH, DH), DH)
    my_rows = pl.ds(pl.multiple_of(c * T, T), T)
    my_halo_rows = pl.ds(pl.multiple_of(WIN + c * T, WIN), T)

    def place(i, s):
        return (kb.at[s, my_halo_rows], vb.at[s, my_halo_rows], qb.at[s, my_rows])[i]

    inputs = (k_ref, v_ref, q_ref)

    def local_in(i, s):
        return pltpu.make_async_copy(inputs[i].at[s, :, my_cols], place(i, s), loc_sem.at[i, s])

    def to_sibling(i, s):
        return remote(
            inputs[i].at[s, :, other_cols], place(i, s), d2d_s.at[i, s], d2d_r.at[i, s], sibling
        )

    w_copies = [
        pltpu.make_async_copy(wg_ref.at[c], w.at[0], w_sem.at[0]),
        pltpu.make_async_copy(wu_ref.at[c], w.at[1], w_sem.at[1]),
        pltpu.make_async_copy(wd_ref.at[c], wdb, w_sem.at[2]),
    ]
    wo_copies = [
        pltpu.make_async_copy(wo_ref.at[:, pl.ds(i * 512, 512)], wo.at[i], wo_sem.at[i]) for i in range(2)
    ]
    rate_load = pltpu.make_async_copy(rate_ref, rate_in, rate_l)
    rate_load.start()
    local_in(0, 0).start()
    w_copies[0].start()
    w_copies[1].start()
    w_copies[2].start()
    local_in(1, 0).start()
    local_in(0, 1).start()
    local_in(1, 1).start()
    local_in(2, 0).start()
    local_in(2, 1).start()
    wo_copies[0].start()
    wo_copies[1].start()

    rate_send[...] = jnp.zeros_like(rate_send)
    rate_load.wait()
    for s in range(SEG):
        both = rate_in[s]
        rates[c, s : s + 1, :] = jnp.where(c == 0, both[0:1], both[1:2])
        rate_send[s : s + 1, :] = jnp.where(c == 0, both[1:2], both[0:1])
    rate_copy = remote(rate_send, rates.at[c], rate_s, rate_r, sibling)

    w_copies[0].wait()
    wb[0] = w[0].astype(BF)
    w_copies[1].wait()
    wb[1] = w[1].astype(BF)
    def forward(s, half, j):
        start = pl.multiple_of(half * T + j * BLK, BLK)
        rows = pl.ds(pl.multiple_of(WIN + start, BLK), BLK)
        cols = pl.ds(start, BLK)
        key = kb[s, rows, :]
        value = vb[s, rows, :]
        rate = -rates[half, s : s + 1, pl.ds(pl.multiple_of(j * BLK, BLK), BLK)]
        g1 = nt(wb[0], key)
        g3 = nt(wb[1], key)
        back = nt(wb[2], value) * rate
        sg = sigmoid(g1)
        ga = g1 * sg
        act[:, cols] = (ga * g3 * rate).astype(BF)
        d1[:, cols] = (back * g3 * (sg + ga * (1.0 - sg))).astype(BF)
        d3[:, cols] = (back * ga).astype(BF)

    def rs(s, job, k):
        m, rows = JOBS[job][0], JOBS[job][2]
        device, p = group8(job, k)
        return remote(
            gb.at[s, m, piece(job, p)],
            rsr.at[s, job, k - 1, pl.ds(0, rows)],
            rs_s.at[s, job, k - 1],
            rs_r.at[s, job, k - 1],
            device,
        )

    def ar(s, job, k):
        ref = arb.at[s, job, group4(job, 0)[1], pl.ds(0, JOBS[job][2])]
        return remote(ref, ref, ar_s.at[s, job, k - 1], ar_r.at[s, job, k - 1], group4(job, k)[0])

    def ag(s, job, k):
        ref = gf.at[s, JOBS[job][0], piece(job, group8(job, 0)[1])]
        return remote(ref, ref, ag_s.at[s, job, k - 1], ag_r.at[s, job, k - 1], group8(job, k)[0])

    far_first = (5, 4, 3, 7, 2, 6, 1)
    order = (2, 0, 1)

    def gradients(s):
        keys = kb[s, pl.ds(WIN, TC), :]
        values = vb[s, pl.ds(WIN, TC), :]
        for m in order:
            grad = nn(act[...], values) if m == 2 else nn((d1, d3)[m][...], keys)
            grad = grad.reshape(16, 32, DH)
            g32[m] = grad
            gb[s, m] = grad.astype(BF)
            for k in far_first:
                for job in range(4):
                    if JOBS[job][0] == m:
                        rs(s, job, k).start()

    def reduce(s):
        for job in range(4):
            m, rows = JOBS[job][0], JOBS[job][2]
            for k in far_first:
                rs(s, job, k).wait()
            total = g32[m, piece(job, group8(job, 0)[1])]
            for k in range(1, 8):
                total = total + rsr[s, job, k - 1, 0:rows].astype(F32)
            arb[s, job, group4(job, 0)[1], 0:rows] = total.astype(BF)
            for k in (3, 2, 1):
                ar(s, job, k).start()

    def spread(s):
        for job in range(4):
            m, rows = JOBS[job][0], JOBS[job][2]
            for k in (1, 2, 3):
                ar(s, job, k).wait()
            total = arb[s, job, 0, 0:rows].astype(F32)
            for a in range(1, 4):
                total = total + arb[s, job, a, 0:rows].astype(F32)
            gf[s, m, piece(job, group8(job, 0)[1])] = total.astype(BF)
            for k in far_first:
                ag(s, job, k).start()

    def arrive(s):
        for job in range(4):
            for k in far_first:
                ag(s, job, k).wait()

    def update(s):
        cur = []
        for m in range(3):
            rows = gf[s, m].reshape(FH, DH).astype(F32)
            norm = jnp.sqrt(jnp.sum(rows * rows, keepdims=True))
            cur.append(rows * (1.0 / (norm + tiny)))
        for i in range(SINGLE_STEPS + SPLIT_STEPS):
            high = [a.astype(BF) for a in cur]
            gram = [tn(a, a) for a in high]
            if i < SINGLE_STEPS:
                gram_b = [a.astype(BF) for a in gram]
                square = [nn(a, a) for a in gram_b]
                mixer = [(coef_b * a + coef_c * b).astype(BF) for a, b in zip(gram, square)]
                change = [nn(a, b) for a, b in zip(high, mixer)]
            else:
                parts = [split(a) for a in gram]
                cross = [nn(a, b) for a, b in parts]
                square = [nn(a, a) + (b + b.T) for (a, _), b in zip(parts, cross)]
                mixer = [split(coef_b * a + coef_c * b) for a, b in zip(gram, square)]
                low = [(a - b.astype(F32)).astype(BF) for a, b in zip(cur, high)]
                change = [nn(a, b) + (nn(a, d) + nn(e, b)) for a, e, (b, d) in zip(high, low, mixer)]
            cur = [coef_a * a + b for a, b in zip(cur, change)]
        step = step_ref[c]
        for m in range(3):
            new = w[m] - step * cur[m]
            w[m] = new
            wb[m] = new.astype(BF)

    row_ids = lax.broadcasted_iota(jnp.int32, (BLK, 2 * BLK), 0)
    col_ids = lax.broadcasted_iota(jnp.int32, (BLK, 2 * BLK), 1)

    def attention(s, j):
        start = pl.multiple_of(j * BLK, BLK)
        query = qb[s, pl.ds(start, BLK), :]
        key = kb[s, pl.ds(start, 2 * BLK), :]
        value = vb[s, pl.ds(start, 2 * BLK), :]
        scores = nt(query, key) * (1.0 / 16.0)
        least = jnp.where(jnp.logical_and(chip == 0, j == 0), WIN, 0)
        allowed = (col_ids > row_ids) & (col_ids <= row_ids + WIN) & (col_ids >= least)
        scores = jnp.where(allowed, scores, -1e30)
        top = jnp.max(scores, axis=-1, keepdims=True)
        weights = jnp.exp(scores - top)
        total = jnp.sum(weights, axis=-1, keepdims=True)
        att[s, pl.ds(start, BLK), :] = nn(weights.astype(BF), value) / total

    def attend(s, first, last):
        def one(j, carry):
            attention(s, j)
            return carry

        lax.fori_loop(first, last, one, 0)

    def fast(s, half, rows):
        start = pl.multiple_of(half * T + rows.start, rows.size)
        query = qb[s, pl.ds(start, rows.size), :]
        g1 = nt(query, wb[0])
        g3 = nt(query, wb[1])
        hidden = (g1 * sigmoid(g1) * g3).astype(BF)
        return (att[s, pl.ds(start, rows.size), :] + nn(hidden, wb[2])).astype(BF)

    def part(s, j):
        return pl.ds(j * ROWS[s], ROWS[s])

    def cs_copy(s, j):
        rows = part(s, j)
        return remote(cs.at[s, rows], cb.at[s, c, rows], cs_s.at[s, j], cs_r.at[s, j], sibling)

    def z_copy(s, j):
        rows = part(s, j)
        return remote(zs.at[s, rows], zr.at[s, rows], zs_s.at[s, j], zs_r.at[s, j], across)

    def project(s, j, group):
        rows = part(s, j)
        return (
            nn(cb[s, 0, rows], wo[group, 0:DH, :]) + nn(cb[s, 1, rows], wo[group, DH : 2 * DH, :])
        ).astype(BF)

    def apply(s):
        count = T // ROWS[s]
        for j in range(count):
            cs[s, part(s, j)] = fast(s, oc, part(s, j))
            cs_copy(s, j).start()
            cb[s, c, part(s, j)] = fast(s, c, part(s, j))
            cs_copy(s, j).wait_recv()
            zs[s, part(s, j)] = project(s, j, 1 - hg)
            z_copy(s, j).start()
        for j in range(count):
            cs_copy(s, j).wait_send()
            zo[s, part(s, j)] = project(s, j, hg)

    def out_copy(s, j):
        rows = part(s, j)
        return pltpu.make_async_copy(mx.at[s, rows], mixed_ref.at[s, rows], out_sem.at[s, j])

    def finish(s):
        for j in range(T // ROWS[s]):
            rows = part(s, j)
            z_copy(s, j).wait()
            mx[s, rows] = (zo[s, rows].astype(F32) + zr[s, rows].astype(F32)).astype(BF)
            out_copy(s, j).start()

    def halo(i, s):
        buf = (kb, vb)[i]
        return remote(
            buf.at[s, pl.ds(TC, WIN)], buf.at[s, pl.ds(0, WIN)], halo_s.at[i, s], halo_r.at[i, s], next_chip
        )

    pl.semaphore_wait(barrier, len(senders))
    to_sibling(0, 0).start()
    to_sibling(1, 0).start()
    rate_copy.start()
    for i, s in ((0, 1), (1, 1), (2, 0), (2, 1)):
        to_sibling(i, s).start()
    w_copies[2].wait()
    w[2] = wdb[...].T
    wb[2] = w[2].astype(BF)
    local_in(0, 0).wait()
    local_in(1, 0).wait()
    forward(0, c, 0)
    forward(0, c, 1)
    to_sibling(0, 0).wait()
    to_sibling(1, 0).wait()
    rate_copy.wait()
    forward(0, oc, 0)
    forward(0, oc, 1)
    gradients(0)

    for i in range(3):
        local_in(i, 1).wait()
        to_sibling(i, 1).wait()
    local_in(2, 0).wait()
    to_sibling(2, 0).wait()
    for i in range(2):
        wo_copies[i].wait()

    reduce(0)
    attend(0, 1, 4)
    spread(0)
    arrive(0)
    halos = [halo(i, s) for s in range(SEG) for i in range(2)]
    for copy in halos:
        copy.start()
    update(0)

    for j in range(2):
        forward(1, c, j)
        forward(1, oc, j)
    gradients(1)
    attend(1, 1, 4)
    reduce(1)
    for copy in halos:
        copy.wait()
    attend(0, 0, 1)
    attend(1, 0, 1)
    spread(1)
    apply(0)
    arrive(1)
    update(1)
    apply(1)

    outs = (gate_ref.at[c], up_ref.at[c], down_ref.at[c])
    wdb[...] = w[2].T
    sources = (w.at[0], w.at[1], wdb)
    for m in range(3):
        remote(sources[m], outs[m], st_s.at[m], st_r.at[m], sibling).start()
        pltpu.make_async_copy(sources[m], outs[m], w_sem.at[m]).start()
    finish(0)
    finish(1)
    for m in range(3):
        remote(sources[m], outs[m], st_s.at[m], st_r.at[m], sibling).wait()
        pltpu.make_async_copy(sources[m], outs[m], w_sem.at[m]).wait()
    for s in range(SEG):
        for j in range(T // ROWS[s]):
            out_copy(s, j).wait()


def deliver(*refs):
    ins, outs, bufs, get_sem, put_sem = refs[0:4], refs[4:8], refs[8:12], refs[12], refs[13]
    gets, puts = [], []
    for i in (1, 2, 3, 0):
        for h in range(2):
            gets.append(pltpu.make_async_copy(ins[i].at[h], bufs[i].at[h], get_sem.at[i, h]))
            puts.append(pltpu.make_async_copy(bufs[i].at[h], outs[i].at[h], put_sem.at[i, h]))
    for get in gets:
        get.start()
    for get, put in zip(gets, puts):
        get.wait()
        put.start()
    for put in puts:
        put.wait()


def body(queries, keys, values, token_rate, step_size, w_gate, w_up, w_down, w_out):
    dma = pltpu.SemaphoreType.DMA
    anywhere = pl.BlockSpec(memory_space=pl.ANY)

    def b16(*shape):
        return pltpu.VMEM(shape, BF)

    def f32(*shape):
        return pltpu.VMEM(shape, F32)

    results = pl.pallas_call(
        kernel,
        out_shape=(
            jax.ShapeDtypeStruct((SEG, T, 2 * DH), BF),
            jax.ShapeDtypeStruct((2, FH, DH), F32),
            jax.ShapeDtypeStruct((2, FH, DH), F32),
            jax.ShapeDtypeStruct((2, DH, FH), F32),
        ),
        in_specs=[
            anywhere, anywhere, anywhere,
            anywhere,
            pl.BlockSpec(memory_space=pltpu.SMEM),
            anywhere, anywhere, anywhere, anywhere,
        ],
        out_specs=(anywhere, anywhere, anywhere, anywhere),
        scratch_shapes=[
            b16(SEG, TC, DH), b16(SEG, WIN + TC, DH), b16(SEG, WIN + TC, DH),
            f32(2, 8, T), f32(SEG, 2, T), f32(8, T),
            f32(3, FH, DH), b16(3, FH, DH), f32(DH, FH), b16(2, 512, 512),
            b16(FH, TC), b16(FH, TC), b16(FH, TC),
            f32(3, 16, 32, DH), b16(SEG, 3, 16, 32, DH), b16(SEG, 4, 7, 2, 32, DH), b16(SEG, 4, 4, 2, 32, DH),
            b16(SEG, 3, 16, 32, DH),
            f32(SEG, TC, DH), b16(SEG, T, DH), b16(SEG, 2, T, DH),
            b16(SEG, T, 512), b16(SEG, T, 512), b16(SEG, T, 512), b16(SEG, T, 512),
            dma((3, 2)), dma((3,)), dma((2,)), dma, dma((3, 2)), dma((3, 2)), dma, dma, dma((2, 2)), dma((2, 2)),
            dma((2, 4, 7)), dma((2, 4, 7)), dma((2, 4, 3)), dma((2, 4, 3)), dma((2, 4, 7)), dma((2, 4, 7)),
            dma((2, 4)), dma((2, 4)), dma((2, 4)), dma((2, 4)), dma((3,)), dma((3,)), dma((2, 4)),
        ],
        compiler_params=pltpu.CompilerParams(
            collective_id=0, has_side_effects=True, vmem_limit_bytes=56 * 2**20
        ),
        name="layer",
    )(queries, keys, values, token_rate, step_size, w_gate, w_up, w_down, w_out)
    return pl.pallas_call(
        deliver,
        out_shape=tuple(jax.ShapeDtypeStruct(a.shape, a.dtype) for a in results),
        in_specs=[anywhere] * 4,
        out_specs=(anywhere,) * 4,
        scratch_shapes=[pltpu.VMEM(a.shape, a.dtype) for a in results] + [dma((4, 2)), dma((4, 2))],
        compiler_params=pltpu.CompilerParams(vmem_limit_bytes=60 * 2**20),
        name="deliver",
    )(*results)


def solution(mesh):
    return jax.shard_map(
        body,
        mesh=mesh,
        in_specs=(
            P(None, "seq", "head"),
            P(None, "seq", "head"),
            P(None, "seq", "head"),
            P(None, "head", "seq"),
            P("head"),
            P("head", None, None),
            P("head", None, None),
            P("head", None, None),
            P("head", None),
        ),
        out_specs=(
            P(None, "seq", "head"),
            P("head", None, None),
            P("head", None, None),
            P("head", None, None),
        ),
        check_vma=False,
    )
```
